256 devices in a mesh: win: 4 (over z_hi, core), hap: 64 (over x, z_lo, y).
Axes of the slice: x: 4, y: 4, z: 8 (z_hi: 2, z_lo: 4; z = z_hi * 4 + z_lo), core: 2. Of those that a mesh axis runs over, the one named last changes fastest.
Arguments:
- queries: bfloat16 [24576, 512], P(('win', 'hap')), parts along dimension 0, may hold values from -6 to 6
- ref_keys: bfloat16 [65536, 512], P(('win', 'hap')), parts along dimension 0, may hold values from -6 to 6
- ref_values: bfloat16 [65536, 512], P(('win', 'hap')), parts along dimension 0, may hold values from -6 to 6
- attn_out: bfloat16 [24576, 512], P(('win', 'hap')), parts along dimension 0, may hold values from -6 to 6
- log_norm: float32 [8, 24576], P(None, ('win', 'hap')), parts along dimension 1, as said below
- w_out: bfloat16 [2048, 256], P('win'), parts along dimension 0, may hold values from -0.25 to 0.25
- dosage_truth: float32 [24576, 256], P(('win', 'hap')), parts along dimension 0, may hold values from -6 to 6
- marker_mask: int32 [1024], P('win'), parts along dimension 0, may hold values 0 or 1
Outputs:
- grad_query: bfloat16 [24576, 512], P(('win', 'hap')), parts along dimension 0
- grad_keys: float32 [65536, 512], P(('win', 'hap')), parts along dimension 0
- grad_values: float32 [65536, 512], P(('win', 'hap')), parts along dimension 0
The draws below stay inside these ranges and needn't reach their ends.
There are 4 independent parts, one for each index of `win`. The reference program is written for one: setup_inputs(seed, part) draws one part's arguments, and reference() takes and returns one part's arrays. A program takes and returns all parts, laid end to end along the dimension named above; each array names one. Nothing has to cross between parts.
Inputs may be any that keep to these rules, and one draw needn't show every extreme that they name: `log_norm`: each entry lies within one unit of ln(16384) + 0.5.
All inputs are finite; a program needn't handle non-finite values.
Results may differ from the reference program's by a relative error of at most 0.019.
Values may be sent and summed in bfloat16 or wider, within the bound.
No kernel may reach another device: no remote copies, remote signals or barrier semaphores. Data moves between devices by JAX's collectives and lax.ppermute only.
A program may use at most 320 MiB of HBM per device.

```python
import jax
import jax.numpy as jnp
from jax import lax

D = 512
H = 8
HD = 64
M = 256
TGT = 6144
REF = 16384


def draw_log_norm(key, part):
    key = jax.random.fold_in(key, 5)
    jitter = jax.random.uniform(key, (H, TGT), jnp.float32, -0.5, 0.5)
    return (jnp.log(jnp.float32(REF)) + 0.5 + jitter).astype(jnp.float32)


def place_ends(result, stream_key, low, largest):
    longest = result.shape.index(max(result.shape))
    spots = []
    for shift in (0, 1):
        where = [jax.random.randint(jax.random.fold_in(stream_key, axis), (), 0, length) for axis, length in enumerate(result.shape)]
        where[longest] = (where[longest] + shift) % result.shape[longest]
        spots.append(tuple(where))
    return result.at[spots[0]].set(low).at[spots[1]].set(largest)


def steps_of(stream_key, shape, shards, low, high):
    def one(axis_at, shards_of):
        steps = jax.random.uniform(jax.random.fold_in(jax.random.fold_in(stream_key, 6), axis_at), (shards_of,), jnp.float32, low / len(shards), high / len(shards))
        return jnp.repeat(jnp.exp(steps), shape[axis_at] // shards_of).reshape((-1,) + (1,) * (len(shape) - axis_at - 1))

    gain = one(*shards[0])
    for cut in shards[1:]:
        gain = gain * one(*cut)
    return gain


def noise(rng, dims, spread, most, cuts=(), dtype=jnp.bfloat16):
    values = spread * jax.random.normal(rng, dims, jnp.float32)
    if cuts:
        values = values * steps_of(rng, dims, cuts, -0.22, 0.18)
    return jnp.clip(values, -most, most).astype(dtype)


def setup_inputs(seed: int = 0, part: int = 0) -> dict:
    splits = jax.random.split(jax.random.key(seed), 9)
    own_keys = jax.random.split(jax.random.fold_in(splits[8], part), 9)
    queries = noise(own_keys[0], (TGT, D), 1.0, 6.0, ((0, 64),))
    ref_keys = noise(own_keys[1], (REF, D), 1.0, 6.0, ((0, 64),))
    ref_values = noise(own_keys[2], (REF, D), 1.0, 6.0, ((0, 64),))
    attn_out = noise(own_keys[3], (TGT, D), 1.0, 6.0, ((0, 64),))
    log_norm = draw_log_norm(jax.random.fold_in(jax.random.fold_in(splits[8], part), 71), part)
    w_out = noise(own_keys[5], (D, M), D ** -0.5, 0.25)
    dosage_truth = noise(own_keys[6], (TGT, M), 1.0, 6.0, ((0, 64),), jnp.float32)
    marker_mask = place_ends((jax.random.randint(own_keys[7], (M,), 0, 2) < 1).astype(jnp.int32), jax.random.fold_in(own_keys[7], 1), 0, 1)
    return {"queries": queries, "ref_keys": ref_keys, "ref_values": ref_values, "attn_out": attn_out, "log_norm": log_norm, "w_out": w_out, "dosage_truth": dosage_truth, "marker_mask": marker_mask}


def reference(queries, ref_keys, ref_values, attn_out, log_norm, w_out, dosage_truth, marker_mask):
    fp = jnp.float32
    scale = (1.0 * HD) ** -0.5
    predicted = jnp.dot(attn_out, w_out, preferred_element_type=fp)
    residue = (marker_mask.astype(fp)[None, :] * (predicted - dosage_truth)).astype(jnp.bfloat16)
    grad_out = jnp.dot(residue, w_out.T, preferred_element_type=fp).astype(jnp.bfloat16)
    delta = jnp.transpose((grad_out.astype(fp) * attn_out.astype(fp)).reshape(TGT, H, HD).sum(-1))
    key_heads = ref_keys.astype(fp).reshape(REF, H, HD)
    value_heads = ref_values.astype(fp).reshape(REF, H, HD)
    tile = min(256, TGT)
    count = TGT // tile
    query_tiles = queries.astype(fp).reshape(count, tile, H, HD)
    grad_tiles = grad_out.astype(fp).reshape(count, tile, H, HD)
    norm_tiles = jnp.transpose(log_norm.reshape(H, count, tile), (1, 0, 2))
    delta_tiles = jnp.transpose(delta.reshape(H, count, tile), (1, 0, 2))

    def advance(carry, inputs):
        key_acc, value_acc = carry
        query_tile, grad_tile, norm_tile, delta_tile = inputs
        scores = jnp.einsum("thd,rhd->htr", query_tile, key_heads) * scale
        probs = jnp.exp(scores - norm_tile[:, :, None])
        probs_low = lax.optimization_barrier(probs.astype(jnp.bfloat16)).astype(fp)
        dprobs = jnp.einsum("thd,rhd->htr", grad_tile, value_heads)
        dscores = (probs * (dprobs - delta_tile[:, :, None]) * scale).astype(jnp.bfloat16)
        dscores = lax.optimization_barrier(dscores).astype(fp)
        query_part = jnp.einsum("htr,rhd->thd", dscores, key_heads)
        key_acc = key_acc + jnp.einsum("htr,thd->rhd", dscores, query_tile)
        value_acc = value_acc + jnp.einsum("htr,thd->rhd", probs_low, grad_tile)
        return (key_acc, value_acc), query_part

    start = jnp.zeros((REF, H, HD), fp)
    (key_acc, value_acc), query_parts = lax.scan(advance, (start, start), (query_tiles, grad_tiles, norm_tiles, delta_tiles))
    grad_query = query_parts.reshape(TGT, D).astype(jnp.bfloat16)
    return grad_query, key_acc.reshape(REF, D), value_acc.reshape(REF, D)
```

```python
import functools

import numpy as np

import jax
import jax.numpy as jnp
from jax import lax
from jax.experimental import pallas as pl
from jax.experimental.pallas import tpu as pltpu
from jax.sharding import PartitionSpec as P

F32 = jnp.float32
BF16 = jnp.bfloat16
AXES = ("win", "hap")
NT = (((1,), (1,)), ((), ()))
NN = (((1,), (0,)), ((), ()))
TN = (((0,), (0,)), ((), ()))
HEADS = 8
HALF = 64
LANES = 128
NORM_PARTS = 3
DELTA_PARTS = 2
RANK = 4


def dot(a, b, dims):
    return lax.dot_general(a, b, dims, preferred_element_type=F32)


def exchange(array, axis, masks):
    pairs = []
    for win in range(RANK):
        mask = masks[win % 2]
        for x in range(RANK):
            for z in range(RANK):
                for y in range(RANK):
                    to = {
                        "x": (x ^ mask, z, y),
                        "z": (x, z ^ mask, y),
                        "y": (x, z, y ^ mask),
                    }[axis]
                    source = win * 64 + x * 16 + z * 4 + y
                    target = win * 64 + to[0] * 16 + to[1] * 4 + to[2]
                    pairs.append((source, target))
    return lax.ppermute(array, AXES, pairs)


X_STEPS = ((1, 3), (3, 1))
Y_STEPS = ((1, 3), (3, 1))
Z_MASKS = (1, 2, 3)
PIECE = 384
T_TILE = 256


def split_parts(value, count):
    parts = []
    for _ in range(count):
        part = value.astype(BF16)
        parts.append(part)
        value = value - part.astype(F32)
    return parts


def place_matrices():
    norm_place = np.zeros((NORM_PARTS * HEADS, LANES), np.float32)
    for row in range(NORM_PARTS * HEADS):
        norm_place[row, row] = 1
    head_sum = np.zeros((HEADS * HALF, LANES), np.float32)
    for feature in range(HEADS * HALF):
        for part in range(DELTA_PARTS):
            head_sum[feature, (NORM_PARTS + part) * HEADS + feature // HALF] = 1
    spread = np.zeros((LANES, HEADS // 2, LANES), np.float32)
    for head in range(HEADS):
        pair, odd = head // 2, head % 2
        first = 0 if odd else HALF
        for part in range(NORM_PARTS + DELTA_PARTS):
            spread[part * HEADS + head, pair, first + part] = 1
    return norm_place, head_sum, spread.reshape(LANES, HEADS // 2 * LANES)


def prologue_kernel(
    queries, attn, w_out, truth, mask, log_norm, norm_place, head_sum, keys, values,
    message, pack,
):
    pack[:, :512] = keys[...]
    pack[:, 512:] = values[...]
    attn_rows = attn[...]
    predicted = dot(attn_rows, w_out[...], NN)
    residue = (mask[...].astype(F32) * (predicted - truth[...])).astype(BF16)
    grad_out = dot(residue, w_out[...], NT).astype(BF16)
    product = grad_out.astype(F32) * attn_rows.astype(F32)
    sums = head_sum[...]
    delta = jnp.zeros((attn_rows.shape[0], LANES), F32)
    for part in split_parts(product, 3):
        delta = delta + dot(part, sums, NN)
    delta = -delta
    delta_high = delta.astype(BF16)
    delta_low = (delta - delta_high.astype(F32)).astype(BF16)
    norm_rows = jnp.concatenate(
        [part.astype(F32) for part in split_parts(-log_norm[...], NORM_PARTS)], 0
    ).astype(BF16)
    norms = dot(norm_rows, norm_place[...], TN)
    lane = lax.broadcasted_iota(jnp.int32, norms.shape, 1)
    deltas = jnp.where(
        lane < (NORM_PARTS + 1) * HEADS, delta_high.astype(F32), delta_low.astype(F32)
    )
    message[:, :512] = queries[...]
    message[:, 512:768] = residue
    message[:, 768:] = (norms + deltas).astype(BF16)


def attention_kernel(tiles, refs, carried, *args):
    count = len(tiles)
    args = list(args)
    take = lambda n: [args.pop(0) for _ in range(n)]
    q_refs, res_refs, st_refs = take(count), take(count), take(count)
    k_refs, v_refs = take(len(refs)), take(len(refs))
    w_out, spread = take(2)
    sums_in = take(2) if carried else None
    gq_outs = take(sum(tiles) // PIECE)
    g_outs = take(len(refs)) if carried else take(2)
    qs, gs, ks, vs, gk_sum, gv_sum = args
    lane = lax.broadcasted_iota(jnp.int32, (1, LANES), 1)
    low = lane < HALF
    place = lane % HALF
    one, zero = jnp.ones((), BF16), jnp.zeros((), BF16)
    norm_lanes = jnp.where(place < NORM_PARTS, one, zero)
    delta_lanes = jnp.where(
        place < NORM_PARTS, zero, jnp.where(place < NORM_PARTS + DELTA_PARTS, one, zero)
    )
    start = 0
    for size, q_ref, res_ref, st_ref in zip(tiles, q_refs, res_refs, st_refs):
        rows = slice(start, start + size)
        start += size
        grads = dot(res_ref[...], w_out[...], NT).astype(BF16)
        extra = dot(st_ref[...], spread[...], NN).astype(BF16)
        query = q_ref[...]
        qs[0, rows, :] = jnp.where(low, query, extra)
        qs[1, rows, :] = jnp.where(low, extra, query)
        gs[0, rows, :] = jnp.where(low, grads, extra)
        gs[1, rows, :] = jnp.where(low, extra, grads)
    start = 0
    for size, k_ref, v_ref in zip(refs, k_refs, v_refs):
        rows = slice(start, start + size)
        start += size
        keys = k_ref[...] * jnp.asarray(0.125, BF16)
        values = v_ref[...]
        ks[0, rows, :] = jnp.where(low, keys, norm_lanes)
        ks[1, rows, :] = jnp.where(low, norm_lanes, keys)
        vs[0, rows, :] = jnp.where(low, values, delta_lanes)
        vs[1, rows, :] = jnp.where(low, delta_lanes, values)
    for first in range(0, sum(tiles), T_TILE):
        rows = slice(first, first + T_TILE)
        gq = []
        for odd in range(2):
            query, grads, keys = qs[odd, rows, :], gs[odd, rows, :], ks[odd]
            probs = jnp.exp(dot(query, keys, NT))
            slopes = (probs * dot(grads, vs[odd], NT)).astype(BF16)
            gq.append(dot(slopes, keys, NN))
            half = slice(odd * HALF, (odd + 1) * HALF)
            key_term = dot(query, slopes, TN)[half]
            value_term = dot(grads, probs.astype(BF16), TN)[half]
            if first:
                gk_sum[half, :] += key_term
                gv_sum[half, :] += value_term
            elif carried:
                gk_sum[half, :] = sums_in[0][half, :] + key_term
                gv_sum[half, :] = sums_in[1][half, :] + value_term
            else:
                gk_sum[half, :] = key_term
                gv_sum[half, :] = value_term
        gq = jnp.where(low, gq[0], gq[1]).astype(BF16)
        at = first
        while at < first + T_TILE:
            piece = at // PIECE
            stop = min(first + T_TILE, (piece + 1) * PIECE)
            gq_outs[piece][at - piece * PIECE : stop - piece * PIECE, :] = gq[
                at - first : stop - first
            ]
            at = stop
    here = pl.multiple_of(pl.program_id(0) * LANES, LANES)
    if not carried:
        g_outs[0][...] = gk_sum[...]
        g_outs[1][...] = gv_sum[...]
        return
    start = 0
    for size, out in zip(refs, g_outs):
        cols = slice(start, start + size)
        start += size
        out[:, pl.ds(here, LANES)] = (gk_sum[:, cols].T * 0.125).astype(BF16)
        out[:, pl.ds(out.shape[1] // 2 + here, LANES)] = gv_sum[:, cols].T.astype(BF16)


def attention(messages, packs, w_out, spread, first, pairs, sums=None):
    carried = sums is not None
    tiles = tuple(m.shape[0] for m in messages)
    refs = tuple(p.shape[0] for p in packs)
    targets, total = sum(tiles), sum(refs)
    spec = pl.BlockSpec
    in_specs = [spec((t, LANES), lambda j: (0, first + j)) for t in tiles]
    in_specs += [spec((t, 256), lambda j: (0, 2)) for t in tiles]
    in_specs += [spec((t, LANES), lambda j: (0, 6)) for t in tiles]
    in_specs += [spec((r, LANES), lambda j: (0, first + j)) for r in refs]
    in_specs += [spec((r, LANES), lambda j: (0, 4 + first + j)) for r in refs]
    in_specs += [
        spec((LANES, 256), lambda j: (first + j, 0)),
        spec((LANES, LANES), lambda j: (0, first + j)),
    ]
    operands = list(messages) * 3 + list(packs) * 2 + [w_out, spread]
    out_specs = [spec((PIECE, LANES), lambda j: (0, j))] * (targets // PIECE)
    out_shape = [jax.ShapeDtypeStruct((PIECE, pairs * LANES), BF16)] * (targets // PIECE)
    if carried:
        in_specs += [spec((LANES, total), lambda j: (first + j, 0))] * 2
        operands += list(sums)
        out_specs += [spec((r, 2 * LANES * pairs), lambda j: (0, 0)) for r in refs]
        out_shape += [jax.ShapeDtypeStruct((r, 2 * LANES * pairs), BF16) for r in refs]
    else:
        out_specs += [spec((LANES, total), lambda j: (j, 0))] * 2
        out_shape += [jax.ShapeDtypeStruct((LANES * pairs, total), F32)] * 2
    return pl.pallas_call(
        functools.partial(attention_kernel, tiles, refs, carried),
        grid=(pairs,),
        in_specs=in_specs,
        out_specs=out_specs,
        out_shape=out_shape,
        scratch_shapes=[
            pltpu.VMEM((2, targets, LANES), BF16),
            pltpu.VMEM((2, targets, LANES), BF16),
            pltpu.VMEM((2, total, LANES), BF16),
            pltpu.VMEM((2, total, LANES), BF16),
            pltpu.VMEM((LANES, total), F32),
            pltpu.VMEM((LANES, total), F32),
        ],
        compiler_params=pltpu.CompilerParams(vmem_limit_bytes=62 * 2**20),
        cost_estimate=pl.CostEstimate(
            flops=40 * targets * total * pairs * LANES, bytes_accessed=2**22, transcendentals=0
        ),
    )(*operands)


def total_of(parts):
    return sum(part.astype(F32) for part in parts).astype(BF16)


def body(queries, ref_keys, ref_values, attn_out, log_norm, w_out, dosage_truth, marker_mask):
    norm_place, head_sum, spread = (jnp.asarray(m, BF16) for m in place_matrices())
    message, pack = pl.pallas_call(
        prologue_kernel,
        out_shape=[
            jax.ShapeDtypeStruct((queries.shape[0], 896), BF16),
            jax.ShapeDtypeStruct((ref_keys.shape[0], 1024), BF16),
        ],
        compiler_params=pltpu.CompilerParams(vmem_limit_bytes=62 * 2**20),
    )(
        queries, attn_out, w_out, dosage_truth, marker_mask[None, :], log_norm,
        norm_place, head_sum, ref_keys, ref_values,
    )
    pack = jnp.concatenate([pack, exchange(pack, "y", Y_STEPS[0])], 0)
    along = [exchange(message, "z", (m, m)) for m in Z_MASKS]
    pack, along[0] = lax.optimization_barrier((pack, along[0]))
    message = jnp.concatenate([message] + along, 0)
    pack_far = exchange(pack, "y", Y_STEPS[1])
    beside = exchange(message, "x", X_STEPS[0])
    both = jnp.concatenate([message, beside], 0)
    far = exchange(both, "x", X_STEPS[1])
    packs = [pack, pack_far]

    gq_mine, gq_beside, *sums = attention([both], packs, w_out, spread, 0, 4)
    back = exchange(gq_beside, "x", X_STEPS[0])
    gq_near, gq_far, near_kv, far_kv = attention([far], packs, w_out, spread, 0, 4, sums)
    back, gq_near, gq_far, far_kv = lax.optimization_barrier((back, gq_near, gq_far, far_kv))
    got_kv = exchange(far_kv, "y", Y_STEPS[1])
    across = exchange(gq_far, "x", (2, 2))
    near = exchange(gq_near, "x", X_STEPS[1])

    gq = total_of([gq_mine, back, near, across])
    half_kv = near_kv.astype(F32) + got_kv.astype(F32)
    refs_here = ref_keys.shape[0]
    other = half_kv[refs_here:].astype(BF16)
    gq, other = lax.optimization_barrier((gq, other))
    quarter = gq.shape[0] // RANK
    part = lambda at: gq[at * quarter : (at + 1) * quarter]
    grad_query = total_of(
        [part(0)]
        + [exchange(part(at + 1), "z", (m, m)) for at, m in enumerate(Z_MASKS)]
    )
    total = half_kv[:refs_here] + exchange(other, "y", Y_STEPS[0]).astype(F32)
    return grad_query, total[:, :512], total[:, 512:]


def solution(mesh):
    rows = P(("win", "hap"), None)
    return jax.shard_map(
        body,
        mesh=mesh,
        in_specs=(
            rows, rows, rows, rows,
            P(None, ("win", "hap")),
            P("win", None),
            rows,
            P("win"),
        ),
        out_specs=(rows, rows, rows),
        check_vma=False,
    )
```

```python
import functools

import numpy as np

import jax
import jax.numpy as jnp
from jax import lax
from jax.experimental import pallas as pl
from jax.experimental.pallas import tpu as pltpu
from jax.sharding import PartitionSpec as P

F32 = jnp.float32
BF16 = jnp.bfloat16
AXES = ("win", "hap")
NT = (((1,), (1,)), ((), ()))
NN = (((1,), (0,)), ((), ()))
TN = (((0,), (0,)), ((), ()))
HEADS = 8
HALF = 64
LANES = 128
NORM_PARTS = 3
DELTA_PARTS = 2
RANK = 4


def dot(a, b, dims):
    return lax.dot_general(a, b, dims, preferred_element_type=F32)


def exchange(array, axis, masks):
    pairs = []
    for win in range(RANK):
        mask = masks[win % 2]
        for x in range(RANK):
            for z in range(RANK):
                for y in range(RANK):
                    to = {
                        "x": (x ^ mask, z, y),
                        "z": (x, z ^ mask, y),
                        "y": (x, z, y ^ mask),
                    }[axis]
                    source = win * 64 + x * 16 + z * 4 + y
                    target = win * 64 + to[0] * 16 + to[1] * 4 + to[2]
                    pairs.append((source, target))
    return lax.ppermute(array, AXES, pairs)


X_STEPS = ((1, 3), (3, 1))
Y_STEPS = ((1, 3), (3, 1))
Z_MASKS = (2, 3, 1)
PIECE = 384
T_TILE = 256
SHARD = 96
GROUP = 32
ROWS = 6 * SHARD + GROUP
STATS = (NORM_PARTS + DELTA_PARTS) * HEADS


def split_parts(value, count):
    parts = []
    for _ in range(count):
        part = value.astype(BF16)
        parts.append(part)
        value = value - part.astype(F32)
    return parts


def place_matrices():
    norm_place = np.zeros((NORM_PARTS * HEADS, LANES), np.float32)
    for row in range(NORM_PARTS * HEADS):
        norm_place[row, row] = 1
    head_sum = np.zeros((HEADS * HALF, LANES), np.float32)
    for feature in range(HEADS * HALF):
        for part in range(DELTA_PARTS):
            head_sum[feature, (NORM_PARTS + part) * HEADS + feature // HALF] = 1
    groups = SHARD // GROUP
    shift = np.zeros((groups, LANES, LANES), np.float32)
    spread = np.zeros((LANES, HEADS // 2, groups, LANES), np.float32)
    for group in range(groups):
        for row in range(STATS):
            shift[group, row, group * STATS + row] = 1
        for head in range(HEADS):
            pair, odd = head // 2, head % 2
            first = 0 if odd else HALF
            for part in range(NORM_PARTS + DELTA_PARTS):
                row = group * STATS + part * HEADS + head
                spread[row, pair, group, first + part] = 1
    return norm_place, head_sum, shift, spread.reshape(LANES, HEADS // 2 * groups * LANES)


def prologue_kernel(
    queries, attn, w_out, truth, mask, log_norm, norm_place, head_sum, shift,
    keys, values, message, pack,
):
    pack[:, :512] = keys[...]
    pack[:, 512:] = values[...]
    attn_rows = attn[...]
    predicted = dot(attn_rows, w_out[...], NN)
    residue = (mask[...].astype(F32) * (predicted - truth[...])).astype(BF16)
    grad_out = dot(residue, w_out[...], NT).astype(BF16)
    product = grad_out.astype(F32) * attn_rows.astype(F32)
    sums = head_sum[...]
    delta = jnp.zeros((attn_rows.shape[0], LANES), F32)
    for part in split_parts(product, 3):
        delta = delta + dot(part, sums, NN)
    delta = -delta
    delta_high = delta.astype(BF16)
    delta_low = (delta - delta_high.astype(F32)).astype(BF16)
    norm_rows = jnp.concatenate(
        [part.astype(F32) for part in split_parts(-log_norm[...], NORM_PARTS)], 0
    ).astype(BF16)
    norms = dot(norm_rows, norm_place[...], TN)
    lane = lax.broadcasted_iota(jnp.int32, norms.shape, 1)
    deltas = jnp.where(
        lane < (NORM_PARTS + 1) * HEADS, delta_high.astype(F32), delta_low.astype(F32)
    )
    stats = (norms + deltas).astype(BF16)
    for pair in range(HEADS // 2):
        message[pair * SHARD : (pair + 1) * SHARD, :] = queries[:, pair * LANES : (pair + 1) * LANES]
    message[4 * SHARD : 5 * SHARD, :] = residue[:, :LANES]
    message[5 * SHARD : 6 * SHARD, :] = residue[:, LANES:]
    packed = sum(
        dot(stats[at * GROUP : (at + 1) * GROUP], shift[at], NN) for at in range(shift.shape[0])
    )
    message[6 * SHARD :, :] = packed.astype(BF16)


def attention_kernel(first_pair, shards, refs, carried, *args):
    targets = shards * SHARD
    args = list(args)
    take = lambda n: [args.pop(0) for _ in range(n)]
    (msg,) = take(1)
    k_refs, v_refs = take(len(refs)), take(len(refs))
    w_out, spread = take(2)
    sums_in = take(2) if carried else None
    gq_outs = take(targets // PIECE)
    g_outs = take(len(refs)) if carried else take(2)
    qs, gs, ks, vs, gk_sum, gv_sum = args
    lane = lax.broadcasted_iota(jnp.int32, (1, LANES), 1)
    low = lane < HALF
    place = lane % HALF
    one, zero = jnp.ones((), BF16), jnp.zeros((), BF16)
    norm_lanes = jnp.where(place < NORM_PARTS, one, zero)
    delta_lanes = jnp.where(
        place < NORM_PARTS, zero, jnp.where(place < NORM_PARTS + DELTA_PARTS, one, zero)
    )
    gather = lambda at, size: jnp.concatenate(
        [msg[m * ROWS + at : m * ROWS + at + size, :] for m in range(shards)], 0
    )
    residue = jnp.concatenate([gather(4 * SHARD, SHARD), gather(5 * SHARD, SHARD)], 1)
    grads = dot(residue, w_out[...], NT).astype(BF16)
    stats = gather(6 * SHARD, GROUP)
    placed = dot(stats, spread[...], NN).astype(BF16)
    groups = [placed[:, at * LANES : (at + 1) * LANES] for at in range(SHARD // GROUP)]
    pair = pl.program_id(0) + first_pair
    for m in range(shards):
        rows = slice(m * SHARD, (m + 1) * SHARD)
        query = msg[pl.ds(pl.multiple_of(m * ROWS + pair * SHARD, GROUP), SHARD), :]
        extra = jnp.concatenate([g[m * GROUP : (m + 1) * GROUP] for g in groups], 0)
        grad = grads[rows]
        qs[0, rows, :] = jnp.where(low, query, extra)
        qs[1, rows, :] = jnp.where(low, extra, query)
        gs[0, rows, :] = jnp.where(low, grad, extra)
        gs[1, rows, :] = jnp.where(low, extra, grad)
    start = 0
    for size, k_ref, v_ref in zip(refs, k_refs, v_refs):
        rows = slice(start, start + size)
        start += size
        keys = k_ref[...] * jnp.asarray(0.125, BF16)
        values = v_ref[...]
        ks[0, rows, :] = jnp.where(low, keys, norm_lanes)
        ks[1, rows, :] = jnp.where(low, norm_lanes, keys)
        vs[0, rows, :] = jnp.where(low, values, delta_lanes)
        vs[1, rows, :] = jnp.where(low, delta_lanes, values)
    for first in range(0, targets, T_TILE):
        rows = slice(first, first + T_TILE)
        gq = []
        for odd in range(2):
            query, grads, keys = qs[odd, rows, :], gs[odd, rows, :], ks[odd]
            probs = jnp.exp(dot(query, keys, NT))
            slopes = (probs * dot(grads, vs[odd], NT)).astype(BF16)
            gq.append(dot(slopes, keys, NN))
            half = slice(odd * HALF, (odd + 1) * HALF)
            key_term = dot(query, slopes, TN)[half]
            value_term = dot(grads, probs.astype(BF16), TN)[half]
            if first:
                gk_sum[half, :] += key_term
                gv_sum[half, :] += value_term
            elif carried:
                gk_sum[half, :] = sums_in[0][half, :] + key_term
                gv_sum[half, :] = sums_in[1][half, :] + value_term
            else:
                gk_sum[half, :] = key_term
                gv_sum[half, :] = value_term
        gq = jnp.where(low, gq[0], gq[1]).astype(BF16)
        at = first
        while at < first + T_TILE:
            piece = at // PIECE
            stop = min(first + T_TILE, (piece + 1) * PIECE)
            gq_outs[piece][at - piece * PIECE : stop - piece * PIECE, :] = gq[
                at - first : stop - first
            ]
            at = stop
    if not carried:
        g_outs[0][...] = gk_sum[...]
        g_outs[1][...] = gv_sum[...]
        return
    start = 0
    for size, out in zip(refs, g_outs):
        cols = slice(start, start + size)
        start += size
        out[:, :LANES] = (gk_sum[:, cols].T * 0.125).astype(BF16)
        out[:, LANES:] = gv_sum[:, cols].T.astype(BF16)


def attention(message, packs, w_out, spread, first, pairs, sums=None):
    carried = sums is not None
    shards = message.shape[0] // ROWS
    refs = tuple(p.shape[0] for p in packs)
    targets, total = shards * SHARD, sum(refs)
    spec = pl.BlockSpec
    in_specs = [spec(message.shape, lambda j: (0, 0))]
    in_specs += [spec((r, LANES), lambda j: (0, first + j)) for r in refs]
    in_specs += [spec((r, LANES), lambda j: (0, 4 + first + j)) for r in refs]
    in_specs += [
        spec((LANES, 256), lambda j: (first + j, 0)),
        spec((LANES, SHARD // GROUP * LANES), lambda j: (0, first + j)),
    ]
    operands = [message] + list(packs) * 2 + [w_out, spread]
    out_specs = [spec((PIECE, LANES), lambda j: (0, j))] * (targets // PIECE)
    out_shape = [jax.ShapeDtypeStruct((PIECE, pairs * LANES), BF16)] * (targets // PIECE)
    if carried:
        in_specs += [spec((LANES, total), lambda j: (first + j, 0))] * 2
        operands += list(sums)
        out_specs += [spec((r, 2 * LANES), lambda j: (0, j)) for r in refs]
        out_shape += [jax.ShapeDtypeStruct((r, 2 * LANES * pairs), BF16) for r in refs]
    else:
        out_specs += [spec((LANES, total), lambda j: (j, 0))] * 2
        out_shape += [jax.ShapeDtypeStruct((LANES * pairs, total), F32)] * 2
    return pl.pallas_call(
        functools.partial(attention_kernel, first, shards, refs, carried),
        grid=(pairs,),
        in_specs=in_specs,
        out_specs=out_specs,
        out_shape=out_shape,
        scratch_shapes=[
            pltpu.VMEM((2, targets, LANES), BF16),
            pltpu.VMEM((2, targets, LANES), BF16),
            pltpu.VMEM((2, total, LANES), BF16),
            pltpu.VMEM((2, total, LANES), BF16),
            pltpu.VMEM((LANES, total), F32),
            pltpu.VMEM((LANES, total), F32),
        ],
        compiler_params=pltpu.CompilerParams(vmem_limit_bytes=62 * 2**20),
        cost_estimate=pl.CostEstimate(
            flops=40 * targets * total * pairs * LANES, bytes_accessed=2**22, transcendentals=0
        ),
    )(*operands)


def split_kernel(near, other, keys_out, values_out):
    total = near[...] + other[...].astype(F32)
    for pair in range(HEADS // 2):
        lanes = slice(pair * LANES, (pair + 1) * LANES)
        keys_out[:, lanes] = total[:, 2 * pair * LANES : (2 * pair + 1) * LANES]
        values_out[:, lanes] = total[:, (2 * pair + 1) * LANES : (2 * pair + 2) * LANES]


def total_of(parts):
    return sum(part.astype(F32) for part in parts).astype(BF16)


def body(queries, ref_keys, ref_values, attn_out, log_norm, w_out, dosage_truth, marker_mask):
    norm_place, head_sum, shift, spread = (jnp.asarray(m, BF16) for m in place_matrices())
    message, pack = pl.pallas_call(
        prologue_kernel,
        out_shape=[
            jax.ShapeDtypeStruct((ROWS, LANES), BF16),
            jax.ShapeDtypeStruct((ref_keys.shape[0], 1024), BF16),
        ],
        compiler_params=pltpu.CompilerParams(vmem_limit_bytes=62 * 2**20),
    )(
        queries, attn_out, w_out, dosage_truth, marker_mask[None, :], log_norm,
        norm_place, head_sum, shift, ref_keys, ref_values,
    )
    pack = jnp.concatenate([pack, exchange(pack, "y", Y_STEPS[0])], 0)
    along = [exchange(message, "z", (m, m)) for m in Z_MASKS]
    pack, along[2] = lax.optimization_barrier((pack, along[2]))
    message = jnp.concatenate([message] + along, 0)
    pack_far = exchange(pack, "y", Y_STEPS[1])
    beside = exchange(message, "x", X_STEPS[0])
    both = jnp.concatenate([message, beside], 0)
    far = exchange(both, "x", X_STEPS[1])
    packs = [pack, pack_far]

    gq_mine, gq_beside, *sums = attention(both, packs, w_out, spread, 0, 4)
    back = exchange(gq_beside, "x", X_STEPS[0])
    gq_near, gq_far, near_kv, far_kv = attention(far, packs, w_out, spread, 0, 4, sums)
    back, gq_near, gq_far, far_kv = lax.optimization_barrier((back, gq_near, gq_far, far_kv))
    got_kv = exchange(far_kv, "y", Y_STEPS[1])
    across = exchange(gq_far, "x", (2, 2))
    near = exchange(gq_near, "x", X_STEPS[1])

    gq = total_of([gq_mine, back, near, across])
    half_kv = near_kv.astype(F32) + got_kv.astype(F32)
    refs_here = ref_keys.shape[0]
    other = half_kv[refs_here:].astype(BF16)
    gq, other = lax.optimization_barrier((gq, other))
    quarter = gq.shape[0] // RANK
    part = lambda at: gq[at * quarter : (at + 1) * quarter]
    grad_query = total_of(
        [part(0)]
        + [exchange(part(at + 1), "z", (m, m)) for at, m in enumerate(Z_MASKS)]
    )
    grad_keys, grad_values = pl.pallas_call(
        split_kernel,
        out_shape=[jax.ShapeDtypeStruct((refs_here, 512), F32)] * 2,
        compiler_params=pltpu.CompilerParams(vmem_limit_bytes=32 * 2**20),
    )(half_kv[:refs_here], exchange(other, "y", Y_STEPS[0]))
    return grad_query, grad_keys, grad_values


def solution(mesh):
    rows = P(("win", "hap"), None)
    return jax.shard_map(
        body,
        mesh=mesh,
        in_specs=(
            rows, rows, rows, rows,
            P(None, ("win", "hap")),
            P("win", None),
            rows,
            P("win"),
        ),
        out_specs=(rows, rows, rows),
        check_vma=False,
    )
```
